32 devices in a mesh: wide: 8 (over z, y), narrow: 4 (over x, core).
Axes of the slice: x: 2, y: 2, z: 4, core: 2. Of those that a mesh axis runs over, the one named last changes fastest.
Arguments:
- tau: float32 [512, 40000], P(None, 'narrow'), may hold values from -6 to 6
- vv_integrals: float32 [40000, 1024], P('narrow', 'wide'), may hold values from -0.03125 to 0.03125
- cycle_amps: float32 [512, 12000], P('wide', 'narrow'), may hold values from -6 to 6
- ov_integrals: float32 [12000, 1024], P('narrow', 'wide'), may hold values from -0.0546875 to 0.0546875
Outputs:
- ladder_residual: float32 [512, 1024], P('narrow', 'wide')
- cycle_residual: float32 [512, 1024], P('narrow', 'wide')
The draws below stay inside these ranges and needn't reach their ends.
All inputs are finite; a program needn't handle non-finite values.
Results may differ from the reference program's by a relative error of at most 0.000071.
Values sent between devices are 32-bit elements; how exact they have to be, the bound alone decides.
A program may use at most 64 MiB of HBM per device.

```python
import jax
import jax.numpy as jnp
from jax import lax

O = 60
V = 200
ROWS = 512
AB = 1024
JB = 1024
PAIRS = 40000
OV = 12000


def spiked(drawn, own_key, source, target, shards_of, factor):
    owner, partner = [(jnp.arange(drawn.shape[position]) // (drawn.shape[position] // shards_of)).reshape([-1 if axis == position else 1 for axis in range(drawn.ndim)]) for position in (source, target)]
    chosen = jax.random.permutation(own_key, shards_of)[partner]
    strong = (owner == chosen) | (owner == (partner + shards_of // 2) % shards_of)
    return jnp.where(strong, factor * drawn, drawn)


def level_of(own_key, dims, split, low, high):
    def one(dim, shards_of):
        draws = jax.random.uniform(jax.random.fold_in(jax.random.fold_in(own_key, 6), dim), (shards_of,), jnp.float32, low / len(split), high / len(split))
        return jnp.repeat(jnp.exp(draws), dims[dim] // shards_of).reshape((-1,) + (1,) * (len(dims) - dim - 1))

    level = one(*split[0])
    for cut in split[1:]:
        level = level * one(*cut)
    return level


def centred(own_key, shape, width, bound, cuts=(), kind=jnp.bfloat16):
    result = jax.random.normal(own_key, shape, jnp.float32) * width
    if len(cuts) > 0:
        result = level_of(own_key, shape, cuts, -0.22, 0.18) * result
    return jnp.clip(result, min=-bound, max=bound).astype(kind)


def bell_draw_with(stream_key, extent, spread, most, shards, heavy, dtype=jnp.bfloat16):
    values = spread * jax.random.normal(stream_key, extent, jnp.float32)
    if shards:
        values = values * level_of(stream_key, extent, shards, -0.22, 0.18)
    return jnp.clip(spiked(values, jax.random.fold_in(stream_key, 3), *heavy), -most, most).astype(dtype)


def setup_inputs(seed: int = 0) -> dict:
    streams_of = jax.random.split(jax.random.key(seed), 5)
    tau = bell_draw_with(streams_of[0], (ROWS, PAIRS), 1.0, 6.0, ((1, 4),), (1, 0, 4, 2.0), jnp.float32)
    vv_integrals = centred(streams_of[1], (PAIRS, AB), (V * V) ** -0.5, 0.03125, ((0, 4), (1, 8)), jnp.float32)
    cycle_amps = bell_draw_with(streams_of[2], (ROWS, OV), 1.0, 6.0, ((0, 8), (1, 4)), (1, 0, 8, 2.0), jnp.float32)
    ov_integrals = centred(streams_of[3], (OV, JB), (O * V) ** -0.5, 0.0546875, ((0, 4), (1, 8)), jnp.float32)
    return {"tau": tau, "vv_integrals": vv_integrals, "cycle_amps": cycle_amps, "ov_integrals": ov_integrals}


def reference(tau, vv_integrals, cycle_amps, ov_integrals):
    ladder_residual = jnp.dot(tau, vv_integrals, precision=lax.Precision.HIGHEST, preferred_element_type=jnp.float32)
    cycle_residual = jnp.dot(cycle_amps, ov_integrals, precision=lax.Precision.HIGHEST, preferred_element_type=jnp.float32)
    return ladder_residual, cycle_residual
```

```python
import functools

import jax
import jax.numpy as jnp
from jax import lax
from jax.experimental import pallas as pl
from jax.experimental.pallas import tpu as pltpu
from jax.sharding import PartitionSpec as P

MESH = pl.DeviceIdType.MESH
F32 = jnp.float32
BF16 = jnp.bfloat16
STEP_Y = 4


def halves(x):
    hi = x.astype(BF16)
    lo = (x - hi.astype(F32)).astype(BF16)
    return hi, lo


def dot(a, b):
    return jnp.dot(a, b, preferred_element_type=F32)


def kernel(depth, tk, steps, kh,
           tau_ref, vv_ref, amps_ref, ov_ref, lad_ref, cyc_ref,
           a_buf, a_send, b_buf, b_send, b_hi, b_lo, acc, part, rs_c, rs_l,
           zr_send, zl_send, a_recv, y_send, b_recv, c_send, c_recv, l_send, l_recv):
    s = pl.program_id(0)
    w, n = lax.axis_index("wide"), lax.axis_index("narrow")
    z = w // 2
    y = w - 2 * z
    yp = 2 * z + 1 - y
    cols = ov_ref.shape[1]
    rows = amps_ref.shape[0]
    own = amps_ref.shape[1]
    rest = own - kh

    def a_copy(zs, j, dz):
        send = zr_send if dz > 0 else zl_send
        return pltpu.make_async_remote_copy(
            src_ref=a_buf.at[zs, j], dst_ref=a_buf.at[zs, j], send_sem=send.at[zs, j],
            recv_sem=a_recv.at[zs, j], device_id=(w + 2 * dz, n), device_id_type=MESH)

    def ya_copy():
        return pltpu.make_async_remote_copy(
            src_ref=a_send, dst_ref=a_buf.at[z, 1], send_sem=y_send.at[0],
            recv_sem=a_recv.at[z, 1], device_id=(yp, n), device_id_type=MESH)

    def yb_copy():
        return pltpu.make_async_remote_copy(
            src_ref=b_send, dst_ref=b_buf.at[1], send_sem=y_send.at[1],
            recv_sem=b_recv, device_id=(yp, n), device_id_type=MESH)

    def c_copy(zs, j, slot):
        return pltpu.make_async_remote_copy(
            src_ref=part.at[zs, j], dst_ref=rs_c.at[slot, j], send_sem=c_send.at[zs, j],
            recv_sem=c_recv.at[slot, j], device_id=(w if j == 0 else yp, zs), device_id_type=MESH)

    def l_copy(zs, slot):
        return pltpu.make_async_remote_copy(
            src_ref=acc.at[pl.ds(zs * 128, 128)], dst_ref=rs_l.at[slot], send_sem=l_send.at[zs],
            recv_sem=l_recv.at[slot], device_id=(w, zs), device_id_type=MESH)

    @pl.when(s == 0)
    def _():
        barrier = pltpu.get_barrier_semaphore()
        for k in range(4):
            @pl.when(n != k)
            def _():
                pl.semaphore_signal(barrier, inc=1, device_id=(w, k), device_id_type=MESH)
            pl.semaphore_signal(barrier, inc=1, device_id=(yp, k), device_id_type=MESH)

        @pl.when(z > 0)
        def _():
            pl.semaphore_signal(barrier, inc=1, device_id=(w - 2, n), device_id_type=MESH)

        @pl.when(z < 3)
        def _():
            pl.semaphore_signal(barrier, inc=1, device_id=(w + 2, n), device_id_type=MESH)

        tail = kh - 128

        @pl.when(y == 0)
        def _():
            a_buf[z, 0] = amps_ref[:, :kh]
            a_send[:, tail:] = jnp.zeros((rows, 128), F32)
            a_send[:, :rest] = amps_ref[:, kh:own]

        @pl.when(y == 1)
        def _():
            a_buf[z, 0, :, tail:] = jnp.zeros((rows, 128), F32)
            a_buf[z, 0, :, :rest] = amps_ref[:, kh:own]
            a_send[...] = amps_ref[:, :kh]

        @pl.when((z == 0) | (z == 3))
        def _():
            pl.semaphore_wait(barrier, 8)

        @pl.when((z == 1) | (z == 2))
        def _():
            pl.semaphore_wait(barrier, 9)

        ya_copy().start()

        @pl.when(z < 3)
        def _():
            a_copy(z, 0, 1).start()

        @pl.when(z > 0)
        def _():
            a_copy(z, 0, -1).start()

        @pl.when(y == 0)
        def _():
            b_buf[0] = ov_ref[:kh]
            b_send[:rest] = ov_ref[kh:own]
            b_send[rest:] = jnp.zeros((kh - rest, cols), F32)

        @pl.when(y == 1)
        def _():
            b_buf[0, :rest] = ov_ref[kh:own]
            b_buf[0, rest:] = jnp.zeros((kh - rest, cols), F32)
            b_send[...] = ov_ref[:kh]

        acc[...] = jnp.zeros(acc.shape, F32)

    @pl.when(s == STEP_Y)
    def _():
        ya_copy().wait_recv()

        @pl.when(z < 3)
        def _():
            a_copy(z, 1, 1).start()

        @pl.when(z > 0)
        def _():
            a_copy(z, 1, -1).start()

        yb_copy().start()

    def ladder(a, b):
        ah, al = halves(a)
        bh, bl = halves(b)
        both = dot(ah, jnp.concatenate([bh, bl], axis=1))
        acc[...] += both[:, :cols] + both[:, cols:] + dot(al, bh)

    @pl.when(s < steps - 1)
    def _():
        ladder(tau_ref[...], vv_ref[...])

    def row_block(zs):
        ah, al = halves(a_buf[zs].reshape(2 * rows, kh))
        r = dot(ah, b_hi[...]) + dot(ah, b_lo[...]) + dot(al, b_hi[...])
        mine = pl.ds(pl.multiple_of(y * rows, rows), rows)
        other = pl.ds(pl.multiple_of((1 - y) * rows, rows), rows)
        for j in range(2):
            part[zs, j, mine, :] = r[:rows, j * cols:(j + 1) * cols]
            part[zs, j, other, :] = r[rows:, j * cols:(j + 1) * cols]

        @pl.when(zs != n)
        def _():
            c_copy(zs, 0, n).start()
        c_copy(zs, 1, n).start()

    def arrive(d, j):
        @pl.when(z >= d)
        def _():
            a_copy(z - d, j, 1).wait_recv()
            if d < 3:
                @pl.when(z < 3)
                def _():
                    a_copy(z - d, j, 1).start()

        @pl.when(z + d <= 3)
        def _():
            a_copy(z + d, j, -1).wait_recv()
            if d < 3:
                @pl.when(z > 0)
                def _():
                    a_copy(z + d, j, -1).start()

    def left_block(d):
        @pl.when(z >= d)
        def _():
            row_block(z - d)

    def right_block(d):
        @pl.when(z + d <= 3)
        def _():
            row_block(z + d)

    @pl.when(s == steps - 1)
    def _():
        last = depth - (steps - 1) * tk
        a = tau_ref[...]
        a = jnp.where(lax.broadcasted_iota(jnp.int32, a.shape, 1) < last, a, 0.0)
        b = vv_ref[...]
        b = jnp.where(lax.broadcasted_iota(jnp.int32, b.shape, 0) < last, b, 0.0)
        ladder(a, b)
        arrive(1, 0)
        for k in range(4):
            @pl.when(n != k)
            def _():
                l_copy(k, n).start()
        arrive(1, 1)
        yb_copy().wait_recv()
        for j in range(2):
            hi, lo = halves(b_buf[j])
            b_hi[:, j * cols:(j + 1) * cols] = hi
            b_lo[:, j * cols:(j + 1) * cols] = lo
        row_block(z)
        arrive(2, 0)
        left_block(1)
        right_block(1)
        arrive(2, 1)
        left_block(2)
        right_block(2)
        total = acc[pl.ds(pl.multiple_of(n * 128, 128), 128), :]
        for k in range(4):
            @pl.when(n != k)
            def _():
                l_copy(k, k).wait_recv()
                l_copy(k, n).wait_send()

            @pl.when(n == k)
            def _():
                rs_l[k] = jnp.zeros((128, cols), F32)
            total += rs_l[k]
        lad_ref[...] = total
        arrive(3, 0)
        arrive(3, 1)
        left_block(3)
        right_block(3)
        total = part[n, 0]
        for k in range(4):
            @pl.when(n != k)
            def _():
                c_copy(k, 0, k).wait_recv()
                c_copy(k, 0, n).wait_send()

            @pl.when(n == k)
            def _():
                rs_c[k, 0] = jnp.zeros((128, cols), F32)
            c_copy(k, 1, k).wait_recv()
            c_copy(k, 1, n).wait_send()
            total += rs_c[k, 0] + rs_c[k, 1]
        cyc_ref[...] = total
        ya_copy().wait_send()
        yb_copy().wait_send()
        for j in range(2):
            for k in range(4):
                @pl.when((z < 3) & (z >= k))
                def _():
                    a_copy(k, j, 1).wait_send()

                @pl.when((z > 0) & (z <= k))
                def _():
                    a_copy(k, j, -1).wait_send()


def fused(tau, vv_integrals, cycle_amps, ov_integrals):
    depth = tau.shape[1]
    cols = vv_integrals.shape[1]
    rows, own = cycle_amps.shape
    kh = -(-own // 256) * 128
    tk = 1280
    steps = -(-depth // tk)
    sem = pltpu.SemaphoreType.DMA
    out = jax.ShapeDtypeStruct((128, cols), F32)
    return pl.pallas_call(
        functools.partial(kernel, depth, tk, steps, kh),
        grid=(steps,),
        out_shape=(out, out),
        in_specs=[
            pl.BlockSpec((tau.shape[0], tk), lambda s: (0, s)),
            pl.BlockSpec((tk, cols), lambda s: (s, 0)),
            pl.BlockSpec((rows, own), lambda s: (0, 0)),
            pl.BlockSpec((own, cols), lambda s: (0, 0)),
        ],
        out_specs=(pl.BlockSpec((128, cols), lambda s: (0, 0)), pl.BlockSpec((128, cols), lambda s: (0, 0))),
        scratch_shapes=[
            pltpu.VMEM((4, 2, rows, kh), F32),
            pltpu.VMEM((rows, kh), F32),
            pltpu.VMEM((2, kh, cols), F32),
            pltpu.VMEM((kh, cols), F32),
            pltpu.VMEM((kh, 2 * cols), BF16),
            pltpu.VMEM((kh, 2 * cols), BF16),
            pltpu.VMEM((512, cols), F32),
            pltpu.VMEM((4, 2, 128, cols), F32),
            pltpu.VMEM((4, 2, 128, cols), F32),
            pltpu.VMEM((4, 128, cols), F32),
            sem((4, 2)), sem((4, 2)), sem((4, 2)), sem((2,)), sem,
            sem((4, 2)), sem((4, 2)), sem((4,)), sem((4,)),
        ],
        compiler_params=pltpu.CompilerParams(
            collective_id=0, has_side_effects=True, vmem_limit_bytes=56 * 1024 * 1024,
            dimension_semantics=("arbitrary",)),
        cost_estimate=pl.CostEstimate(flops=6 * 512 * depth * cols, bytes_accessed=4 * 512 * depth, transcendentals=0),
    )(tau, vv_integrals, cycle_amps, ov_integrals)


def contract(left, right):
    return jnp.dot(left, right, precision=lax.Precision.HIGHEST, preferred_element_type=F32)


def plain(tau, vv_integrals, cycle_amps, ov_integrals):
    ladder_terms = contract(tau, vv_integrals)
    ladder_residual = lax.psum_scatter(ladder_terms, "narrow", scatter_dimension=0, tiled=True)
    cycle_terms = contract(lax.all_gather(cycle_amps, "wide", axis=0, tiled=True), ov_integrals)
    cycle_residual = lax.psum_scatter(cycle_terms, "narrow", scatter_dimension=0, tiled=True)
    return (ladder_residual, cycle_residual)


def solution(mesh):
    in_specs = (P(None, "narrow"), P("narrow", "wide"), P("wide", "narrow"), P("narrow", "wide"))
    out_specs = (P("narrow", "wide"), P("narrow", "wide"))
    small = mesh.shape["wide"] == 8 and mesh.shape["narrow"] == 4
    return jax.shard_map(fused if small else plain, mesh=mesh, in_specs=in_specs, out_specs=out_specs, check_vma=False)
```

```python
import functools

import jax
import jax.numpy as jnp
from jax import lax
from jax.experimental import pallas as pl
from jax.experimental.pallas import tpu as pltpu
from jax.sharding import PartitionSpec as P

MESH = pl.DeviceIdType.MESH
F32 = jnp.float32
BF16 = jnp.bfloat16
STEP_Y = 4


def halves(x):
    hi = x.astype(BF16)
    lo = (x - hi.astype(F32)).astype(BF16)
    return hi, lo


def dot(a, b):
    return jnp.dot(a, b, preferred_element_type=F32)


def kernel(depth, tk, steps, kh,
           tau_ref, vv_ref, amps_ref, ov_ref, out_ref,
           a_buf, a_send, b_buf, b_send, b_hi, b_lo, acc_t, acc, part, rs_c, rs_l,
           zr_send, zl_send, a_recv, y_send, b_recv, c_send, c_recv, l_send, l_recv):
    s = pl.program_id(0)
    w, n = lax.axis_index("wide"), lax.axis_index("narrow")
    z = w // 2
    y = w - 2 * z
    yp = 2 * z + 1 - y
    cols = ov_ref.shape[1]
    rows = amps_ref.shape[0]
    own = amps_ref.shape[1]
    rest = own - kh

    def a_copy(zs, j, dz):
        send = zr_send if dz > 0 else zl_send
        return pltpu.make_async_remote_copy(
            src_ref=a_buf.at[zs, j], dst_ref=a_buf.at[zs, j], send_sem=send.at[zs, j],
            recv_sem=a_recv.at[zs, j], device_id=(w + 2 * dz, n), device_id_type=MESH)

    def ya_copy():
        return pltpu.make_async_remote_copy(
            src_ref=a_send, dst_ref=a_buf.at[z, 1], send_sem=y_send.at[0],
            recv_sem=a_recv.at[z, 1], device_id=(yp, n), device_id_type=MESH)

    def yb_copy():
        return pltpu.make_async_remote_copy(
            src_ref=b_send, dst_ref=b_buf.at[1], send_sem=y_send.at[1],
            recv_sem=b_recv, device_id=(yp, n), device_id_type=MESH)

    def c_copy(zs, j, slot):
        return pltpu.make_async_remote_copy(
            src_ref=part.at[zs, j], dst_ref=rs_c.at[slot, j], send_sem=c_send.at[zs, j],
            recv_sem=c_recv.at[slot, j], device_id=(w if j == 0 else yp, zs), device_id_type=MESH)

    def l_copy(zs, slot):
        return pltpu.make_async_remote_copy(
            src_ref=acc.at[pl.ds(zs * 128, 128)], dst_ref=rs_l.at[slot], send_sem=l_send.at[zs],
            recv_sem=l_recv.at[slot], device_id=(w, zs), device_id_type=MESH)

    @pl.when(s == 0)
    def _():
        barrier = pltpu.get_barrier_semaphore()
        for k in range(4):
            @pl.when(n != k)
            def _():
                pl.semaphore_signal(barrier, inc=1, device_id=(w, k), device_id_type=MESH)
            pl.semaphore_signal(barrier, inc=1, device_id=(yp, k), device_id_type=MESH)

        @pl.when(z > 0)
        def _():
            pl.semaphore_signal(barrier, inc=1, device_id=(w - 2, n), device_id_type=MESH)

        @pl.when(z < 3)
        def _():
            pl.semaphore_signal(barrier, inc=1, device_id=(w + 2, n), device_id_type=MESH)

        tail = kh - 128

        @pl.when(y == 0)
        def _():
            a_buf[z, 0] = amps_ref[:, :kh]
            a_send[:, tail:] = jnp.zeros((rows, 128), F32)
            a_send[:, :rest] = amps_ref[:, kh:own]

        @pl.when(y == 1)
        def _():
            a_buf[z, 0, :, tail:] = jnp.zeros((rows, 128), F32)
            a_buf[z, 0, :, :rest] = amps_ref[:, kh:own]
            a_send[...] = amps_ref[:, :kh]

        @pl.when((z == 0) | (z == 3))
        def _():
            pl.semaphore_wait(barrier, 8)

        @pl.when((z == 1) | (z == 2))
        def _():
            pl.semaphore_wait(barrier, 9)

        ya_copy().start()

        @pl.when(z < 3)
        def _():
            a_copy(z, 0, 1).start()

        @pl.when(z > 0)
        def _():
            a_copy(z, 0, -1).start()

        @pl.when(y == 0)
        def _():
            b_buf[0] = ov_ref[:kh]
            b_send[:rest] = ov_ref[kh:own]
            b_send[rest:] = jnp.zeros((kh - rest, cols), F32)

        @pl.when(y == 1)
        def _():
            b_buf[0, :rest] = ov_ref[kh:own]
            b_buf[0, rest:] = jnp.zeros((kh - rest, cols), F32)
            b_send[...] = ov_ref[:kh]

        acc_t[...] = jnp.zeros(acc_t.shape, F32)

    @pl.when(s == STEP_Y)
    def _():
        ya_copy().wait_recv()

        @pl.when(z < 3)
        def _():
            a_copy(z, 1, 1).start()

        @pl.when(z > 0)
        def _():
            a_copy(z, 1, -1).start()

        yb_copy().start()

    def ladder(a, b):
        ah, al = halves(a)
        bh, bl = halves(b.T)
        both = dot(jnp.concatenate([bh, bl], axis=0), ah)
        acc_t[...] += both[:cols] + both[cols:] + dot(bh, al)

    @pl.when(s < steps - 1)
    def _():
        ladder(tau_ref[...], vv_ref[...])

    def row_block(zs):
        ah, al = halves(a_buf[zs].reshape(2 * rows, kh))
        r = dot(ah, b_hi[...]) + dot(ah, b_lo[...]) + dot(al, b_hi[...])
        mine = pl.ds(pl.multiple_of(y * rows, rows), rows)
        other = pl.ds(pl.multiple_of((1 - y) * rows, rows), rows)
        for j in range(2):
            part[zs, j, mine, :] = r[:rows, j * cols:(j + 1) * cols]
            part[zs, j, other, :] = r[rows:, j * cols:(j + 1) * cols]

        @pl.when(zs != n)
        def _():
            c_copy(zs, 0, n).start()
        c_copy(zs, 1, n).start()

    def arrive(d, j):
        @pl.when(z >= d)
        def _():
            a_copy(z - d, j, 1).wait_recv()
            if d < 3:
                @pl.when(z < 3)
                def _():
                    a_copy(z - d, j, 1).start()

        @pl.when(z + d <= 3)
        def _():
            a_copy(z + d, j, -1).wait_recv()
            if d < 3:
                @pl.when(z > 0)
                def _():
                    a_copy(z + d, j, -1).start()

    def left_block(d):
        @pl.when(z >= d)
        def _():
            row_block(z - d)

    def right_block(d):
        @pl.when(z + d <= 3)
        def _():
            row_block(z + d)

    @pl.when(s == steps - 1)
    def _():
        last = depth - (steps - 1) * tk
        a = tau_ref[...]
        a = jnp.where(lax.broadcasted_iota(jnp.int32, a.shape, 0) < last, a, 0.0)
        b = vv_ref[...]
        b = jnp.where(lax.broadcasted_iota(jnp.int32, b.shape, 0) < last, b, 0.0)
        ladder(a, b)
        acc[...] = acc_t[...].T
        arrive(1, 0)
        for k in range(4):
            @pl.when(n != k)
            def _():
                l_copy(k, n).start()
        arrive(1, 1)
        yb_copy().wait_recv()
        for j in range(2):
            hi, lo = halves(b_buf[j])
            b_hi[:, j * cols:(j + 1) * cols] = hi
            b_lo[:, j * cols:(j + 1) * cols] = lo
        row_block(z)
        arrive(2, 0)
        left_block(1)
        right_block(1)
        arrive(2, 1)
        left_block(2)
        right_block(2)
        total = acc[pl.ds(pl.multiple_of(n * 128, 128), 128), :]
        for k in range(4):
            @pl.when(n != k)
            def _():
                l_copy(k, k).wait_recv()
                l_copy(k, n).wait_send()

            @pl.when(n == k)
            def _():
                rs_l[k] = jnp.zeros((128, cols), F32)
            total += rs_l[k]
        out_ref[0] = total
        arrive(3, 0)
        arrive(3, 1)
        left_block(3)
        right_block(3)
        total = part[n, 0]
        for k in range(4):
            @pl.when(n != k)
            def _():
                c_copy(k, 0, k).wait_recv()
                c_copy(k, 0, n).wait_send()

            @pl.when(n == k)
            def _():
                rs_c[k, 0] = jnp.zeros((128, cols), F32)
            c_copy(k, 1, k).wait_recv()
            c_copy(k, 1, n).wait_send()
            total += rs_c[k, 0] + rs_c[k, 1]
        out_ref[1] = total
        ya_copy().wait_send()
        yb_copy().wait_send()
        for j in range(2):
            for k in range(4):
                @pl.when((z < 3) & (z >= k))
                def _():
                    a_copy(k, j, 1).wait_send()

                @pl.when((z > 0) & (z <= k))
                def _():
                    a_copy(k, j, -1).wait_send()


def fused(tau, vv_integrals, cycle_amps, ov_integrals):
    depth = tau.shape[1]
    cols = vv_integrals.shape[1]
    rows, own = cycle_amps.shape
    kh = -(-own // 256) * 128
    tk = 1280
    steps = -(-depth // tk)
    sem = pltpu.SemaphoreType.DMA
    both = pl.pallas_call(
        functools.partial(kernel, depth, tk, steps, kh),
        grid=(steps,),
        out_shape=jax.ShapeDtypeStruct((2, 128, cols), F32),
        in_specs=[
            pl.BlockSpec((tk, tau.shape[0]), lambda s: (s, 0)),
            pl.BlockSpec((tk, cols), lambda s: (s, 0)),
            pl.BlockSpec((rows, own), lambda s: (0, 0)),
            pl.BlockSpec((own, cols), lambda s: (0, 0)),
        ],
        out_specs=pl.BlockSpec((2, 128, cols), lambda s: (0, 0, 0)),
        scratch_shapes=[
            pltpu.VMEM((4, 2, rows, kh), F32),
            pltpu.VMEM((rows, kh), F32),
            pltpu.VMEM((2, kh, cols), F32),
            pltpu.VMEM((kh, cols), F32),
            pltpu.VMEM((kh, 2 * cols), BF16),
            pltpu.VMEM((kh, 2 * cols), BF16),
            pltpu.VMEM((cols, 512), F32),
            pltpu.VMEM((512, cols), F32),
            pltpu.VMEM((4, 2, 128, cols), F32),
            pltpu.VMEM((4, 2, 128, cols), F32),
            pltpu.VMEM((4, 128, cols), F32),
            sem((4, 2)), sem((4, 2)), sem((4, 2)), sem((2,)), sem,
            sem((4, 2)), sem((4, 2)), sem((4,)), sem((4,)),
        ],
        compiler_params=pltpu.CompilerParams(
            collective_id=0, has_side_effects=True, vmem_limit_bytes=56 * 1024 * 1024,
            dimension_semantics=("arbitrary",)),
        cost_estimate=pl.CostEstimate(flops=6 * 512 * depth * cols, bytes_accessed=4 * 512 * depth, transcendentals=0),
    )(tau.T, vv_integrals, cycle_amps, ov_integrals)
    return both[0], both[1]


def contract(left, right):
    return jnp.dot(left, right, precision=lax.Precision.HIGHEST, preferred_element_type=F32)


def plain(tau, vv_integrals, cycle_amps, ov_integrals):
    ladder_terms = contract(tau, vv_integrals)
    ladder_residual = lax.psum_scatter(ladder_terms, "narrow", scatter_dimension=0, tiled=True)
    cycle_terms = contract(lax.all_gather(cycle_amps, "wide", axis=0, tiled=True), ov_integrals)
    cycle_residual = lax.psum_scatter(cycle_terms, "narrow", scatter_dimension=0, tiled=True)
    return (ladder_residual, cycle_residual)


def solution(mesh):
    in_specs = (P(None, "narrow"), P("narrow", "wide"), P("wide", "narrow"), P("narrow", "wide"))
    out_specs = (P("narrow", "wide"), P("narrow", "wide"))
    small = mesh.shape["wide"] == 8 and mesh.shape["narrow"] == 4
    return jax.shard_map(fused if small else plain, mesh=mesh, in_specs=in_specs, out_specs=out_specs, check_vma=False)
```

```python
import functools

import jax
import jax.numpy as jnp
from jax import lax
from jax.experimental import pallas as pl
from jax.experimental.pallas import tpu as pltpu
from jax.sharding import PartitionSpec as P

MESH = pl.DeviceIdType.MESH
F32 = jnp.float32
BF16 = jnp.bfloat16


def halves(x):
    hi = x.astype(BF16)
    lo = (x - hi.astype(F32)).astype(BF16)
    return hi, lo


def dot(a, b):
    return jnp.dot(a, b, preferred_element_type=F32)


def kernel(depth, tk, steps, kp, kq,
           tau_ref, vv_ref, amps_ref, ov_ref, out_ref,
           a_p, a_q, as_p, as_q, b_p, b_q, bs_p, bs_q, be_q, b_hi, b_lo, e_hi, e_lo,
           acc_t, acc, part, part_e, rs_c, rs_e, rs_l, fin_s, fin_r,
           sp_e, sp_x, sq_e, sq_x, rp, rq, y_send, yb_recv, be_send, be_recv,
           c_send, c_recv, e_send, e_recv, l_send, l_recv, f_send, f_recv):
    s = pl.program_id(0)
    w, n = lax.axis_index("wide"), lax.axis_index("narrow")
    z = w // 2
    y = w - 2 * z
    yp = 2 * z + 1 - y
    zn = z + 1 - 2 * (z % 2)
    zx = 3 - z
    zxn = 3 - zn
    end = (z == 0) | (z == 3)
    mid = (z == 1) | (z == 2)
    wn = w + 2 * (zn - z)
    wx = w + 2 * (zx - z)
    cols = ov_ref.shape[1]
    rows = amps_ref.shape[0]
    own = amps_ref.shape[1]
    kh = kp + kq
    left = own - kh - kp

    def remote(src, dst, send, recv, wt, nt):
        return pltpu.make_async_remote_copy(
            src_ref=src, dst_ref=dst, send_sem=send, recv_sem=recv, device_id=(wt, nt), device_id_type=MESH)

    def pe(zs, j):
        return remote(a_p.at[zs, j], a_p.at[zs, j], sp_e.at[zs, j], rp.at[zs, j], wn, n)

    def px(zs, j):
        return remote(a_p.at[zs, j], a_p.at[zs, j], sp_x.at[zs, j], rp.at[zs, j], wx, n)

    def qe(zs, j):
        return remote(a_q.at[zs, j], a_q.at[zs, j], sq_e.at[zs, j], rq.at[zs, j], wn, n)

    def qx(zs, j):
        return remote(a_q.at[zs, j], a_q.at[zs, j], sq_x.at[zs, j], rq.at[zs, j], wx, n)

    def ya_p():
        return remote(as_p, a_p.at[z, 1], y_send.at[0], rp.at[z, 1], yp, n)

    def ya_q():
        return remote(as_q, a_q.at[z, 1], y_send.at[1], rq.at[z, 1], yp, n)

    def yb_p():
        return remote(bs_p, b_p.at[1], y_send.at[2], yb_recv.at[0], yp, n)

    def yb_q():
        return remote(bs_q, b_q.at[1], y_send.at[3], yb_recv.at[1], yp, n)

    def be(j):
        return remote(b_q.at[j], be_q.at[j], be_send.at[j], be_recv.at[j], wn, n)

    def c_copy(zs, j, slot):
        return remote(part.at[zs, j], rs_c.at[slot, j], c_send.at[zs, j], c_recv.at[slot, j],
                      w if j == 0 else yp, zs)

    def e_copy(zs, j, slot):
        return remote(part_e.at[zs, j], rs_e.at[slot, j], e_send.at[zs, j], e_recv.at[slot, j],
                      w if j == 0 else yp, zs)

    def l_copy(zs, slot):
        return remote(acc.at[pl.ds(zs * 128, 128)], rs_l.at[slot], l_send.at[zs], l_recv.at[slot], w, zs)

    def f_copy():
        return remote(fin_s, fin_r, f_send, f_recv, wn, n)

    @pl.when(s == 0)
    def _():
        barrier = pltpu.get_barrier_semaphore()
        for k in range(4):
            @pl.when(n != k)
            def _():
                pl.semaphore_signal(barrier, inc=1, device_id=(w, k), device_id_type=MESH)
            pl.semaphore_signal(barrier, inc=1, device_id=(yp, k), device_id_type=MESH)
        pl.semaphore_signal(barrier, inc=1, device_id=(wn, n), device_id_type=MESH)

        @pl.when(mid)
        def _():
            pl.semaphore_signal(barrier, inc=1, device_id=(wx, n), device_id_type=MESH)

        zero = jnp.zeros((rows, 128), F32)

        @pl.when(y == 0)
        def _():
            a_p[z, 0] = amps_ref[:, :kp]
            a_q[z, 0] = amps_ref[:, kp:kh]
            as_p[...] = amps_ref[:, kh:kh + kp]
            as_q[:, kq - 128:] = zero
            as_q[:, :left] = amps_ref[:, kh + kp:own]

        @pl.when(y == 1)
        def _():
            as_p[...] = amps_ref[:, :kp]
            as_q[...] = amps_ref[:, kp:kh]
            a_p[z, 0] = amps_ref[:, kh:kh + kp]
            a_q[z, 0, :, kq - 128:] = zero
            a_q[z, 0, :, :left] = amps_ref[:, kh + kp:own]

        @pl.when(end)
        def _():
            pl.semaphore_wait(barrier, 8)

        @pl.when(mid)
        def _():
            pl.semaphore_wait(barrier, 9)

        ya_p().start()
        ya_q().start()
        pe(z, 0).start()

        @pl.when(end)
        def _():
            qe(z, 0).start()

        @pl.when(mid)
        def _():
            px(z, 0).start()
            qx(z, 0).start()

        pad = jnp.zeros((kq - left, cols), F32)

        @pl.when(y == 0)
        def _():
            b_p[0] = ov_ref[:kp]
            b_q[0] = ov_ref[kp:kh]
            bs_p[...] = ov_ref[kh:kh + kp]
            bs_q[:left] = ov_ref[kh + kp:own]
            bs_q[left:] = pad

        @pl.when(y == 1)
        def _():
            bs_p[...] = ov_ref[:kp]
            bs_q[...] = ov_ref[kp:kh]
            b_p[0] = ov_ref[kh:kh + kp]
            b_q[0, :left] = ov_ref[kh + kp:own]
            b_q[0, left:] = pad

        acc_t[...] = jnp.zeros(acc_t.shape, F32)

    @pl.when((s == 3) & mid)
    def _():
        pe(zn, 0).wait_recv()
        px(zn, 0).start()

    @pl.when(s == 4)
    def _():
        ya_p().wait_recv()
        pe(z, 1).start()

        @pl.when(mid)
        def _():
            px(z, 1).start()

    @pl.when(s == 5)
    def _():
        ya_q().wait_recv()

        @pl.when(end)
        def _():
            qe(z, 1).start()
            be(0).start()

        yb_q().start()
        yb_p().start()

        @pl.when(mid)
        def _():
            qe(zn, 0).wait_recv()
            qx(zn, 0).start()
            px(zx, 0).wait_recv()
            pe(zx, 0).start()

    def ladder(a, b):
        ah, al = halves(a)
        bh, bl = halves(b.T)
        both = dot(jnp.concatenate([bh, bl], axis=0), ah)
        acc_t[...] += both[:cols] + both[cols:] + dot(bh, al)

    @pl.when(s < steps - 1)
    def _():
        ladder(tau_ref[...], vv_ref[...])

    def split_b(ref, hi_ref, lo_ref, at, size):
        for j in range(2):
            hi, lo = halves(ref[j])
            hi_ref[at:at + size, j * cols:(j + 1) * cols] = hi
            lo_ref[at:at + size, j * cols:(j + 1) * cols] = lo

    def three(a, hi, lo):
        ah, al = halves(a.reshape(2 * rows, a.shape[-1]))
        return dot(ah, hi) + dot(ah, lo) + dot(al, hi)

    def place(r, ref, zs, copy):
        mine = pl.ds(pl.multiple_of(y * rows, rows), rows)
        other = pl.ds(pl.multiple_of((1 - y) * rows, rows), rows)
        for j in range(2):
            ref[zs, j, mine, :] = r[:rows, j * cols:(j + 1) * cols]
            ref[zs, j, other, :] = r[rows:, j * cols:(j + 1) * cols]

        @pl.when(zs != n)
        def _():
            copy(zs, 0, n).start()
        copy(zs, 1, n).start()

    def end_block(zs):
        place(three(a_p[zs], b_hi[:kp], b_lo[:kp]), part, zs, c_copy)

    def mid_block(zs):
        r = three(a_p[zs], b_hi[:kp], b_lo[:kp]) + three(a_q[zs], b_hi[kp:], b_lo[kp:])
        place(r, part, zs, c_copy)

    def far_block(zs):
        place(three(a_q[zs], e_hi[...], e_lo[...]), part_e, zs, e_copy)

    def gathered(ref, slots, copy):
        total = ref[n, 0]
        for k in range(4):
            @pl.when(n != k)
            def _():
                copy(k, 0, k).wait_recv()
                copy(k, 0, n).wait_send()

            @pl.when(n == k)
            def _():
                slots[k, 0] = jnp.zeros((128, cols), F32)
            copy(k, 1, k).wait_recv()
            copy(k, 1, n).wait_send()
            total += slots[k, 0] + slots[k, 1]
        return total

    def ladder_out():
        total = acc[pl.ds(pl.multiple_of(n * 128, 128), 128), :]
        for k in range(4):
            @pl.when(n != k)
            def _():
                l_copy(k, k).wait_recv()
                l_copy(k, n).wait_send()

            @pl.when(n == k)
            def _():
                rs_l[k] = jnp.zeros((128, cols), F32)
            total += rs_l[k]
        out_ref[0] = total

    @pl.when(s == steps - 1)
    def _():
        last = depth - (steps - 1) * tk
        a = tau_ref[...]
        a = jnp.where(lax.broadcasted_iota(jnp.int32, a.shape, 0) < last, a, 0.0)
        b = vv_ref[...]
        b = jnp.where(lax.broadcasted_iota(jnp.int32, b.shape, 0) < last, b, 0.0)
        ladder(a, b)

        @pl.when(mid)
        def _():
            pe(zn, 1).wait_recv()
            px(zn, 1).start()
            qx(z, 1).start()
            px(zxn, 0).wait_recv()
            pe(zxn, 0).start()
            px(zx, 1).wait_recv()
            pe(zx, 1).start()
            qe(zn, 1).wait_recv()
            qx(zn, 1).start()

        acc[...] = acc_t[...].T
        for k in range(4):
            @pl.when(n != k)
            def _():
                l_copy(k, n).start()

        yb_q().wait_recv()

        @pl.when(end)
        def _():
            be(1).start()

        split_b(b_q, b_hi, b_lo, kp, kq)
        yb_p().wait_recv()
        split_b(b_p, b_hi, b_lo, 0, kp)

        @pl.when(end)
        def _():
            end_block(z)
            for j in range(2):
                pe(zn, j).wait_recv()
            end_block(zn)
            for j in range(2):
                pe(zx, j).wait_recv()
            ladder_out()
            for j in range(2):
                pe(zxn, j).wait_recv()
            end_block(zxn)
            end_block(zx)
            total = gathered(part, rs_c, c_copy)
            f_copy().wait_recv()
            out_ref[1] = total + fin_r[...]
            for j in range(2):
                pe(z, j).wait_send()
                qe(z, j).wait_send()
                be(j).wait_send()

        @pl.when(mid)
        def _():
            px(zxn, 1).wait_recv()
            pe(zxn, 1).start()
            mid_block(z)
            mid_block(zn)
            for j in range(2):
                qx(zx, j).wait_recv()
            mid_block(zx)
            ladder_out()
            for j in range(2):
                be(j).wait_recv()
            split_b(be_q, e_hi, e_lo, 0, kq)
            far_block(z)
            far_block(zn)
            far_block(zx)
            for j in range(2):
                qx(zxn, j).wait_recv()
            far_block(zxn)
            mid_block(zxn)
            fin_s[...] = gathered(part_e, rs_e, e_copy)
            f_copy().start()
            out_ref[1] = gathered(part, rs_c, c_copy)
            for j in range(2):
                for k in (z, zx, zxn):
                    pe(k, j).wait_send()
                for k in (z, zn):
                    px(k, j).wait_send()
                    qx(k, j).wait_send()
            f_copy().wait_send()

        ya_p().wait_send()
        ya_q().wait_send()
        yb_p().wait_send()
        yb_q().wait_send()


def fused(tau, vv_integrals, cycle_amps, ov_integrals):
    depth = tau.shape[1]
    cols = vv_integrals.shape[1]
    rows, own = cycle_amps.shape
    tiles = -(-own // 256)
    kp = (tiles * 7 // 12) * 128
    kq = tiles * 128 - kp
    kh = kp + kq
    tk = 1280
    steps = -(-depth // tk)
    sem = pltpu.SemaphoreType.DMA
    both = pl.pallas_call(
        functools.partial(kernel, depth, tk, steps, kp, kq),
        grid=(steps,),
        out_shape=jax.ShapeDtypeStruct((2, 128, cols), F32),
        in_specs=[
            pl.BlockSpec((tk, tau.shape[0]), lambda s: (s, 0)),
            pl.BlockSpec((tk, cols), lambda s: (s, 0)),
            pl.BlockSpec((rows, own), lambda s: (0, 0)),
            pl.BlockSpec((own, cols), lambda s: (0, 0)),
        ],
        out_specs=pl.BlockSpec((2, 128, cols), lambda s: (0, 0, 0)),
        scratch_shapes=[
            pltpu.VMEM((4, 2, rows, kp), F32),
            pltpu.VMEM((4, 2, rows, kq), F32),
            pltpu.VMEM((rows, kp), F32),
            pltpu.VMEM((rows, kq), F32),
            pltpu.VMEM((2, kp, cols), F32),
            pltpu.VMEM((2, kq, cols), F32),
            pltpu.VMEM((kp, cols), F32),
            pltpu.VMEM((kq, cols), F32),
            pltpu.VMEM((2, kq, cols), F32),
            pltpu.VMEM((kh, 2 * cols), BF16),
            pltpu.VMEM((kh, 2 * cols), BF16),
            pltpu.VMEM((kq, 2 * cols), BF16),
            pltpu.VMEM((kq, 2 * cols), BF16),
            pltpu.VMEM((cols, 512), F32),
            pltpu.VMEM((512, cols), F32),
            pltpu.VMEM((4, 2, 128, cols), F32),
            pltpu.VMEM((4, 2, 128, cols), F32),
            pltpu.VMEM((4, 2, 128, cols), F32),
            pltpu.VMEM((4, 2, 128, cols), F32),
            pltpu.VMEM((4, 128, cols), F32),
            pltpu.VMEM((128, cols), F32),
            pltpu.VMEM((128, cols), F32),
            sem((4, 2)), sem((4, 2)), sem((4, 2)), sem((4, 2)), sem((4, 2)), sem((4, 2)),
            sem((4,)), sem((2,)), sem((2,)), sem((2,)),
            sem((4, 2)), sem((4, 2)), sem((4, 2)), sem((4, 2)), sem((4,)), sem((4,)), sem, sem,
        ],
        compiler_params=pltpu.CompilerParams(
            collective_id=0, has_side_effects=True, vmem_limit_bytes=56 * 1024 * 1024,
            dimension_semantics=("arbitrary",)),
        cost_estimate=pl.CostEstimate(flops=6 * 512 * depth * cols, bytes_accessed=4 * 512 * depth, transcendentals=0),
    )(tau.T, vv_integrals, cycle_amps, ov_integrals)
    return both[0], both[1]


def contract(left, right):
    return jnp.dot(left, right, precision=lax.Precision.HIGHEST, preferred_element_type=F32)


def plain(tau, vv_integrals, cycle_amps, ov_integrals):
    ladder_terms = contract(tau, vv_integrals)
    ladder_residual = lax.psum_scatter(ladder_terms, "narrow", scatter_dimension=0, tiled=True)
    cycle_terms = contract(lax.all_gather(cycle_amps, "wide", axis=0, tiled=True), ov_integrals)
    cycle_residual = lax.psum_scatter(cycle_terms, "narrow", scatter_dimension=0, tiled=True)
    return (ladder_residual, cycle_residual)


def solution(mesh):
    in_specs = (P(None, "narrow"), P("narrow", "wide"), P("wide", "narrow"), P("narrow", "wide"))
    out_specs = (P("narrow", "wide"), P("narrow", "wide"))
    small = mesh.shape["wide"] == 8 and mesh.shape["narrow"] == 4
    return jax.shard_map(fused if small else plain, mesh=mesh, in_specs=in_specs, out_specs=out_specs, check_vma=False)
```

```python
import functools

import jax
import jax.numpy as jnp
from jax import lax
from jax.experimental import pallas as pl
from jax.experimental.pallas import tpu as pltpu
from jax.sharding import PartitionSpec as P

MESH = pl.DeviceIdType.MESH
F32 = jnp.float32
BF16 = jnp.bfloat16


def halves(x):
    hi = x.astype(BF16)
    lo = (x - hi.astype(F32)).astype(BF16)
    return hi, lo


def dot(a, b):
    return jnp.dot(a, b, preferred_element_type=F32)


def kernel(depth, tk, steps, kp, kq,
           tau_ref, vv_ref, amps_ref, ov_ref, out_ref,
           a_p, a_q, as_p, as_q, b_p, b_q, bs_p, bs_q, be_q, b_hi, b_lo, e_hi, e_lo,
           acc_t, acc, part, part_e, rs_c, rs_e, rs_l, fin_s, fin_r,
           sp_e, sp_x, sq_e, sq_x, rp, rq, y_send, yb_recv, be_send, be_recv,
           c_send, c_recv, e_send, e_recv, l_send, l_recv, f_send, f_recv):
    s = pl.program_id(0)
    w, n = lax.axis_index("wide"), lax.axis_index("narrow")
    z = w // 2
    y = w - 2 * z
    yp = 2 * z + 1 - y
    zn = z + 1 - 2 * (z % 2)
    zx = 3 - z
    zxn = 3 - zn
    end = (z == 0) | (z == 3)
    mid = (z == 1) | (z == 2)
    wn = w + 2 * (zn - z)
    wx = w + 2 * (zx - z)
    cols = ov_ref.shape[1]
    rows = amps_ref.shape[0]
    own = amps_ref.shape[1]
    kh = kp + kq
    left = own - kh - kp

    def remote(src, dst, send, recv, wt, nt):
        return pltpu.make_async_remote_copy(
            src_ref=src, dst_ref=dst, send_sem=send, recv_sem=recv, device_id=(wt, nt), device_id_type=MESH)

    def pe(zs, j):
        return remote(a_p.at[zs, j], a_p.at[zs, j], sp_e.at[zs, j], rp.at[zs, j], wn, n)

    def px(zs, j):
        return remote(a_p.at[zs, j], a_p.at[zs, j], sp_x.at[zs, j], rp.at[zs, j], wx, n)

    def qe(zs, j):
        return remote(a_q.at[zs, j], a_q.at[zs, j], sq_e.at[zs, j], rq.at[zs, j], wn, n)

    def qx(zs, j):
        return remote(a_q.at[zs, j], a_q.at[zs, j], sq_x.at[zs, j], rq.at[zs, j], wx, n)

    def ya_p():
        return remote(as_p, a_p.at[z, 1], y_send.at[0], rp.at[z, 1], yp, n)

    def ya_q():
        return remote(as_q, a_q.at[z, 1], y_send.at[1], rq.at[z, 1], yp, n)

    def yb_p():
        return remote(bs_p, b_p.at[1], y_send.at[2], yb_recv.at[0], yp, n)

    def yb_q():
        return remote(bs_q, b_q.at[1], y_send.at[3], yb_recv.at[1], yp, n)

    def be(j):
        return remote(b_q.at[j], be_q.at[j], be_send.at[j], be_recv.at[j], wn, n)

    def c_copy(zs, j, slot):
        return remote(part.at[zs, j], rs_c.at[slot, j], c_send.at[zs, j], c_recv.at[slot, j],
                      w if j == 0 else yp, zs)

    def e_copy(zs, j, slot):
        return remote(part_e.at[zs, j], rs_e.at[slot, j], e_send.at[zs, j], e_recv.at[slot, j],
                      w if j == 0 else yp, zs)

    def l_copy(zs, slot):
        return remote(acc.at[pl.ds(zs * 128, 128)], rs_l.at[slot], l_send.at[zs], l_recv.at[slot], w, zs)

    def f_copy():
        return remote(fin_s, fin_r, f_send, f_recv, wn, n)

    @pl.when(s == 0)
    def _():
        barrier = pltpu.get_barrier_semaphore()
        for k in range(4):
            @pl.when(n != k)
            def _():
                pl.semaphore_signal(barrier, inc=1, device_id=(w, k), device_id_type=MESH)
            pl.semaphore_signal(barrier, inc=1, device_id=(yp, k), device_id_type=MESH)
        pl.semaphore_signal(barrier, inc=1, device_id=(wn, n), device_id_type=MESH)

        @pl.when(mid)
        def _():
            pl.semaphore_signal(barrier, inc=1, device_id=(wx, n), device_id_type=MESH)

        zero = jnp.zeros((rows, 128), F32)

        @pl.when(y == 0)
        def _():
            a_p[z, 0] = amps_ref[:, :kp]
            a_q[z, 0] = amps_ref[:, kp:kh]
            as_p[...] = amps_ref[:, kh:kh + kp]
            as_q[:, kq - 128:] = zero
            as_q[:, :left] = amps_ref[:, kh + kp:own]

        @pl.when(y == 1)
        def _():
            as_p[...] = amps_ref[:, :kp]
            as_q[...] = amps_ref[:, kp:kh]
            a_p[z, 0] = amps_ref[:, kh:kh + kp]
            a_q[z, 0, :, kq - 128:] = zero
            a_q[z, 0, :, :left] = amps_ref[:, kh + kp:own]

        @pl.when(end)
        def _():
            pl.semaphore_wait(barrier, 8)

        @pl.when(mid)
        def _():
            pl.semaphore_wait(barrier, 9)

        ya_p().start()
        ya_q().start()
        pe(z, 0).start()

        @pl.when(end)
        def _():
            qe(z, 0).start()

        @pl.when(mid)
        def _():
            px(z, 0).start()
            qx(z, 0).start()

        pad = jnp.zeros((kq - left, cols), F32)

        @pl.when(y == 0)
        def _():
            b_p[0] = ov_ref[:kp]
            b_q[0] = ov_ref[kp:kh]
            bs_p[...] = ov_ref[kh:kh + kp]
            bs_q[:left] = ov_ref[kh + kp:own]
            bs_q[left:] = pad

        @pl.when(y == 1)
        def _():
            bs_p[...] = ov_ref[:kp]
            bs_q[...] = ov_ref[kp:kh]
            b_p[0] = ov_ref[kh:kh + kp]
            b_q[0, :left] = ov_ref[kh + kp:own]
            b_q[0, left:] = pad

        acc_t[...] = jnp.zeros(acc_t.shape, F32)

    @pl.when((s == 1) & mid)
    def _():
        pe(zn, 0).wait_recv()
        px(zn, 0).start()

    @pl.when(s == 2)
    def _():
        ya_p().wait_recv()
        pe(z, 1).start()

        @pl.when(mid)
        def _():
            px(z, 1).start()
            px(zx, 0).wait_recv()
            pe(zx, 0).start()

        ya_q().wait_recv()
        yb_q().start()
        yb_p().start()

        @pl.when(end)
        def _():
            qe(z, 1).start()
            be(0).start()

        @pl.when(mid)
        def _():
            qx(z, 1).start()

    @pl.when((s == 3) & mid)
    def _():
        qe(zn, 0).wait_recv()
        qx(zn, 0).start()

    @pl.when((s == 4) & mid)
    def _():
        pe(zn, 1).wait_recv()
        px(zn, 1).start()
        px(zxn, 0).wait_recv()
        pe(zxn, 0).start()

    @pl.when((s == 5) & mid)
    def _():
        px(zx, 1).wait_recv()
        pe(zx, 1).start()

    @pl.when((s == 6) & mid)
    def _():
        qe(zn, 1).wait_recv()
        qx(zn, 1).start()

    def ladder(a, b):
        ah, al = halves(a)
        bh, bl = halves(b.T)
        both = dot(jnp.concatenate([bh, bl], axis=0), ah)
        acc_t[...] += both[:cols] + both[cols:] + dot(bh, al)

    @pl.when(s < steps - 1)
    def _():
        ladder(tau_ref[...], vv_ref[...])

    def split_b(ref, hi_ref, lo_ref, at, size):
        for j in range(2):
            hi, lo = halves(ref[j])
            hi_ref[at:at + size, j * cols:(j + 1) * cols] = hi
            lo_ref[at:at + size, j * cols:(j + 1) * cols] = lo

    def three(a, hi, lo):
        ah, al = halves(a.reshape(2 * rows, a.shape[-1]))
        return dot(ah, hi) + dot(ah, lo) + dot(al, hi)

    def place(r, ref, zs, copy):
        mine = pl.ds(pl.multiple_of(y * rows, rows), rows)
        other = pl.ds(pl.multiple_of((1 - y) * rows, rows), rows)
        for j in range(2):
            ref[zs, j, mine, :] = r[:rows, j * cols:(j + 1) * cols]
            ref[zs, j, other, :] = r[rows:, j * cols:(j + 1) * cols]

        @pl.when(zs != n)
        def _():
            copy(zs, 0, n).start()
        copy(zs, 1, n).start()

    def end_block(zs):
        place(three(a_p[zs], b_hi[:kp], b_lo[:kp]), part, zs, c_copy)

    def mid_block(zs):
        r = three(a_p[zs], b_hi[:kp], b_lo[:kp]) + three(a_q[zs], b_hi[kp:], b_lo[kp:])
        place(r, part, zs, c_copy)

    def far_block(zs):
        place(three(a_q[zs], e_hi[...], e_lo[...]), part_e, zs, e_copy)

    def gathered(ref, slots, copy):
        total = ref[n, 0]
        for k in range(4):
            @pl.when(n != k)
            def _():
                copy(k, 0, k).wait_recv()
                copy(k, 0, n).wait_send()

            @pl.when(n == k)
            def _():
                slots[k, 0] = jnp.zeros((128, cols), F32)
            copy(k, 1, k).wait_recv()
            copy(k, 1, n).wait_send()
            total += slots[k, 0] + slots[k, 1]
        return total

    def ladder_out():
        total = acc[pl.ds(pl.multiple_of(n * 128, 128), 128), :]
        for k in range(4):
            @pl.when(n != k)
            def _():
                l_copy(k, k).wait_recv()
                l_copy(k, n).wait_send()

            @pl.when(n == k)
            def _():
                rs_l[k] = jnp.zeros((128, cols), F32)
            total += rs_l[k]
        out_ref[0] = total

    @pl.when(s == steps - 1)
    def _():
        last = depth - (steps - 1) * tk
        a = tau_ref[...]
        a = jnp.where(lax.broadcasted_iota(jnp.int32, a.shape, 0) < last, a, 0.0)
        b = vv_ref[...]
        b = jnp.where(lax.broadcasted_iota(jnp.int32, b.shape, 0) < last, b, 0.0)
        ladder(a, b)

        acc[...] = acc_t[...].T
        for k in range(4):
            @pl.when(n != k)
            def _():
                l_copy(k, n).start()

        yb_q().wait_recv()

        @pl.when(end)
        def _():
            be(1).start()

        split_b(b_q, b_hi, b_lo, kp, kq)
        yb_p().wait_recv()
        split_b(b_p, b_hi, b_lo, 0, kp)

        @pl.when(end)
        def _():
            end_block(z)
            for j in range(2):
                pe(zn, j).wait_recv()
            end_block(zn)
            for j in range(2):
                pe(zx, j).wait_recv()
            ladder_out()
            for j in range(2):
                pe(zxn, j).wait_recv()
            end_block(zxn)
            end_block(zx)
            total = gathered(part, rs_c, c_copy)
            f_copy().wait_recv()
            out_ref[1] = total + fin_r[...]
            for j in range(2):
                pe(z, j).wait_send()
                qe(z, j).wait_send()
                be(j).wait_send()

        @pl.when(mid)
        def _():
            px(zxn, 1).wait_recv()
            pe(zxn, 1).start()
            mid_block(z)
            mid_block(zn)
            for j in range(2):
                qx(zx, j).wait_recv()
            mid_block(zx)
            ladder_out()
            for j in range(2):
                be(j).wait_recv()
            split_b(be_q, e_hi, e_lo, 0, kq)
            far_block(z)
            far_block(zn)
            far_block(zx)
            for j in range(2):
                qx(zxn, j).wait_recv()
            far_block(zxn)
            mid_block(zxn)
            fin_s[...] = gathered(part_e, rs_e, e_copy)
            f_copy().start()
            out_ref[1] = gathered(part, rs_c, c_copy)
            for j in range(2):
                for k in (z, zx, zxn):
                    pe(k, j).wait_send()
                for k in (z, zn):
                    px(k, j).wait_send()
                    qx(k, j).wait_send()
            f_copy().wait_send()

        ya_p().wait_send()
        ya_q().wait_send()
        yb_p().wait_send()
        yb_q().wait_send()


def fused(tau, vv_integrals, cycle_amps, ov_integrals):
    depth = tau.shape[1]
    cols = vv_integrals.shape[1]
    rows, own = cycle_amps.shape
    tiles = -(-own // 256)
    kp = (tiles * 7 // 12) * 128
    kq = tiles * 128 - kp
    kh = kp + kq
    tk = 1280
    steps = -(-depth // tk)
    sem = pltpu.SemaphoreType.DMA
    both = pl.pallas_call(
        functools.partial(kernel, depth, tk, steps, kp, kq),
        grid=(steps,),
        out_shape=jax.ShapeDtypeStruct((2, 128, cols), F32),
        in_specs=[
            pl.BlockSpec((tk, tau.shape[0]), lambda s: (s, 0)),
            pl.BlockSpec((tk, cols), lambda s: (s, 0)),
            pl.BlockSpec((rows, own), lambda s: (0, 0)),
            pl.BlockSpec((own, cols), lambda s: (0, 0)),
        ],
        out_specs=pl.BlockSpec((2, 128, cols), lambda s: (0, 0, 0)),
        scratch_shapes=[
            pltpu.VMEM((4, 2, rows, kp), F32),
            pltpu.VMEM((4, 2, rows, kq), F32),
            pltpu.VMEM((rows, kp), F32),
            pltpu.VMEM((rows, kq), F32),
            pltpu.VMEM((2, kp, cols), F32),
            pltpu.VMEM((2, kq, cols), F32),
            pltpu.VMEM((kp, cols), F32),
            pltpu.VMEM((kq, cols), F32),
            pltpu.VMEM((2, kq, cols), F32),
            pltpu.VMEM((kh, 2 * cols), BF16),
            pltpu.VMEM((kh, 2 * cols), BF16),
            pltpu.VMEM((kq, 2 * cols), BF16),
            pltpu.VMEM((kq, 2 * cols), BF16),
            pltpu.VMEM((cols, 512), F32),
            pltpu.VMEM((512, cols), F32),
            pltpu.VMEM((4, 2, 128, cols), F32),
            pltpu.VMEM((4, 2, 128, cols), F32),
            pltpu.VMEM((4, 2, 128, cols), F32),
            pltpu.VMEM((4, 2, 128, cols), F32),
            pltpu.VMEM((4, 128, cols), F32),
            pltpu.VMEM((128, cols), F32),
            pltpu.VMEM((128, cols), F32),
            sem((4, 2)), sem((4, 2)), sem((4, 2)), sem((4, 2)), sem((4, 2)), sem((4, 2)),
            sem((4,)), sem((2,)), sem((2,)), sem((2,)),
            sem((4, 2)), sem((4, 2)), sem((4, 2)), sem((4, 2)), sem((4,)), sem((4,)), sem, sem,
        ],
        compiler_params=pltpu.CompilerParams(
            collective_id=0, has_side_effects=True, vmem_limit_bytes=56 * 1024 * 1024,
            dimension_semantics=("arbitrary",)),
        cost_estimate=pl.CostEstimate(flops=6 * 512 * depth * cols, bytes_accessed=4 * 512 * depth, transcendentals=0),
    )(tau.T, vv_integrals, cycle_amps, ov_integrals)
    return both[0], both[1]


def contract(left, right):
    return jnp.dot(left, right, precision=lax.Precision.HIGHEST, preferred_element_type=F32)


def plain(tau, vv_integrals, cycle_amps, ov_integrals):
    ladder_terms = contract(tau, vv_integrals)
    ladder_residual = lax.psum_scatter(ladder_terms, "narrow", scatter_dimension=0, tiled=True)
    cycle_terms = contract(lax.all_gather(cycle_amps, "wide", axis=0, tiled=True), ov_integrals)
    cycle_residual = lax.psum_scatter(cycle_terms, "narrow", scatter_dimension=0, tiled=True)
    return (ladder_residual, cycle_residual)


def solution(mesh):
    in_specs = (P(None, "narrow"), P("narrow", "wide"), P("wide", "narrow"), P("narrow", "wide"))
    out_specs = (P("narrow", "wide"), P("narrow", "wide"))
    small = mesh.shape["wide"] == 8 and mesh.shape["narrow"] == 4
    return jax.shard_map(fused if small else plain, mesh=mesh, in_specs=in_specs, out_specs=out_specs, check_vma=False)
```

```python
import functools

import jax
import jax.numpy as jnp
from jax import lax
from jax.experimental import pallas as pl
from jax.experimental.pallas import tpu as pltpu
from jax.sharding import PartitionSpec as P

MESH = pl.DeviceIdType.MESH
F32 = jnp.float32
BF16 = jnp.bfloat16


def halves(x):
    hi = x.astype(BF16)
    lo = (x - hi.astype(F32)).astype(BF16)
    return hi, lo


def dot(a, b):
    return jnp.dot(a, b, preferred_element_type=F32)


def kernel(depth, tk, steps, kp, kq,
           tau_ref, vv_ref, amps_ref, ov_ref, out_ref,
           a_p, a_q, as_p, as_q, b_p, b_q, bs_p, bs_q, be_q, b_hi, b_lo, e_hi, e_lo,
           acc_t, acc, part, part_e, rs_c, rs_e, rs_l, fin_s, fin_r,
           sp_e, sp_x, sq_e, sq_x, rp, rq, y_send, yb_recv, be_send, be_recv,
           c_send, c_recv, e_send, e_recv, l_send, l_recv, f_send, f_recv):
    s = pl.program_id(0)
    w, n = lax.axis_index("wide"), lax.axis_index("narrow")
    z = w // 2
    y = w - 2 * z
    yp = 2 * z + 1 - y
    zn = z + 1 - 2 * (z % 2)
    zx = 3 - z
    zxn = 3 - zn
    end = (z == 0) | (z == 3)
    mid = (z == 1) | (z == 2)
    wn = w + 2 * (zn - z)
    wx = w + 2 * (zx - z)
    cols = ov_ref.shape[1]
    rows = amps_ref.shape[0]
    own = amps_ref.shape[1]
    kh = kp + kq
    left = own - kh - kp

    def remote(src, dst, send, recv, wt, nt):
        return pltpu.make_async_remote_copy(
            src_ref=src, dst_ref=dst, send_sem=send, recv_sem=recv, device_id=(wt, nt), device_id_type=MESH)

    def pe(zs, j):
        return remote(a_p.at[zs, j], a_p.at[zs, j], sp_e.at[zs, j], rp.at[zs, j], wn, n)

    def px(zs, j):
        return remote(a_p.at[zs, j], a_p.at[zs, j], sp_x.at[zs, j], rp.at[zs, j], wx, n)

    def qe(zs, j):
        return remote(a_q.at[zs, j], a_q.at[zs, j], sq_e.at[zs, j], rq.at[zs, j], wn, n)

    def qx(zs, j):
        return remote(a_q.at[zs, j], a_q.at[zs, j], sq_x.at[zs, j], rq.at[zs, j], wx, n)

    def ya_p():
        return remote(as_p, a_p.at[z, 1], y_send.at[0], rp.at[z, 1], yp, n)

    def ya_q():
        return remote(as_q, a_q.at[z, 1], y_send.at[1], rq.at[z, 1], yp, n)

    def yb_p():
        return remote(bs_p, b_p.at[1], y_send.at[2], yb_recv.at[0], yp, n)

    def yb_q():
        return remote(bs_q, b_q.at[1], y_send.at[3], yb_recv.at[1], yp, n)

    def be(j):
        return remote(b_q.at[j], be_q.at[j], be_send.at[j], be_recv.at[j], wn, n)

    def c_copy(zs, j, slot):
        return remote(part.at[zs, j], rs_c.at[slot, j], c_send.at[zs, j], c_recv.at[slot, j],
                      w if j == 0 else yp, zs)

    def e_copy(zs, j, slot):
        return remote(part_e.at[zs, j], rs_e.at[slot, j], e_send.at[zs, j], e_recv.at[slot, j],
                      w if j == 0 else yp, zs)

    def l_copy(zs, slot):
        return remote(acc.at[pl.ds(zs * 128, 128)], rs_l.at[slot], l_send.at[zs], l_recv.at[slot], w, zs)

    def f_copy():
        return remote(fin_s, fin_r, f_send, f_recv, wn, n)

    @pl.when(s == 0)
    def _():
        barrier = pltpu.get_barrier_semaphore()
        for k in range(4):
            @pl.when(n != k)
            def _():
                pl.semaphore_signal(barrier, inc=1, device_id=(w, k), device_id_type=MESH)
            pl.semaphore_signal(barrier, inc=1, device_id=(yp, k), device_id_type=MESH)
        pl.semaphore_signal(barrier, inc=1, device_id=(wn, n), device_id_type=MESH)

        @pl.when(mid)
        def _():
            pl.semaphore_signal(barrier, inc=1, device_id=(wx, n), device_id_type=MESH)

        zero = jnp.zeros((rows, 128), F32)

        @pl.when(y == 0)
        def _():
            a_p[z, 0] = amps_ref[:, :kp]
            a_q[z, 0] = amps_ref[:, kp:kh]
            as_p[...] = amps_ref[:, kh:kh + kp]
            as_q[:, kq - 128:] = zero
            as_q[:, :left] = amps_ref[:, kh + kp:own]

        @pl.when(y == 1)
        def _():
            as_p[...] = amps_ref[:, :kp]
            as_q[...] = amps_ref[:, kp:kh]
            a_p[z, 0] = amps_ref[:, kh:kh + kp]
            a_q[z, 0, :, kq - 128:] = zero
            a_q[z, 0, :, :left] = amps_ref[:, kh + kp:own]

        @pl.when(end)
        def _():
            pl.semaphore_wait(barrier, 8)

        @pl.when(mid)
        def _():
            pl.semaphore_wait(barrier, 9)

        ya_p().start()
        ya_q().start()
        pe(z, 0).start()

        @pl.when(end)
        def _():
            qe(z, 0).start()

        @pl.when(mid)
        def _():
            px(z, 0).start()
            qx(z, 0).start()

        pad = jnp.zeros((kq - left, cols), F32)

        @pl.when(y == 0)
        def _():
            b_p[0] = ov_ref[:kp]
            b_q[0] = ov_ref[kp:kh]
            bs_p[...] = ov_ref[kh:kh + kp]
            bs_q[:left] = ov_ref[kh + kp:own]
            bs_q[left:] = pad

        @pl.when(y == 1)
        def _():
            bs_p[...] = ov_ref[:kp]
            bs_q[...] = ov_ref[kp:kh]
            b_p[0] = ov_ref[kh:kh + kp]
            b_q[0, :left] = ov_ref[kh + kp:own]
            b_q[0, left:] = pad

        acc_t[...] = jnp.zeros(acc_t.shape, F32)

    @pl.when((s == 3) & mid)
    def _():
        pe(zn, 0).wait_recv()
        px(zn, 0).start()

    @pl.when(s == 4)
    def _():
        ya_p().wait_recv()
        pe(z, 1).start()

        @pl.when(mid)
        def _():
            px(z, 1).start()

    @pl.when(s == 5)
    def _():
        ya_q().wait_recv()

        @pl.when(end)
        def _():
            qe(z, 1).start()
            be(0).start()

        yb_q().start()
        yb_p().start()

        @pl.when(mid)
        def _():
            qe(zn, 0).wait_recv()
            qx(zn, 0).start()
            px(zx, 0).wait_recv()
            pe(zx, 0).start()

    @pl.when((s == 6) & mid)
    def _():
        pe(zn, 1).wait_recv()
        px(zn, 1).start()
        qx(z, 1).start()
        px(zxn, 0).wait_recv()
        pe(zxn, 0).start()

    @pl.when((s == 7) & mid)
    def _():
        px(zx, 1).wait_recv()
        pe(zx, 1).start()
        qe(zn, 1).wait_recv()
        qx(zn, 1).start()

    def ladder(a, b):
        ah, al = halves(a)
        bh, bl = halves(b.T)
        both = dot(jnp.concatenate([bh, bl], axis=0), ah)
        acc_t[...] += both[:cols] + both[cols:] + dot(bh, al)

    @pl.when(s < steps - 1)
    def _():
        ladder(tau_ref[...], vv_ref[...])

    def split_b(ref, hi_ref, lo_ref, at, size):
        for j in range(2):
            hi, lo = halves(ref[j])
            hi_ref[at:at + size, j * cols:(j + 1) * cols] = hi
            lo_ref[at:at + size, j * cols:(j + 1) * cols] = lo

    def three(a, hi, lo):
        ah, al = halves(a.reshape(2 * rows, a.shape[-1]))
        return dot(ah, hi) + dot(ah, lo) + dot(al, hi)

    def place(r, ref, zs, copy):
        mine = pl.ds(pl.multiple_of(y * rows, rows), rows)
        other = pl.ds(pl.multiple_of((1 - y) * rows, rows), rows)
        for j in range(2):
            ref[zs, j, mine, :] = r[:rows, j * cols:(j + 1) * cols]
            ref[zs, j, other, :] = r[rows:, j * cols:(j + 1) * cols]

        @pl.when(zs != n)
        def _():
            copy(zs, 0, n).start()
        copy(zs, 1, n).start()

    def end_block(zs):
        place(three(a_p[zs], b_hi[:kp], b_lo[:kp]), part, zs, c_copy)

    def mid_block(zs):
        r = three(a_p[zs], b_hi[:kp], b_lo[:kp]) + three(a_q[zs], b_hi[kp:], b_lo[kp:])
        place(r, part, zs, c_copy)

    def far_block(zs):
        place(three(a_q[zs], e_hi[...], e_lo[...]), part_e, zs, e_copy)

    def gathered(ref, slots, copy):
        total = ref[n, 0]
        for k in range(4):
            @pl.when(n != k)
            def _():
                copy(k, 0, k).wait_recv()
                copy(k, 0, n).wait_send()

            @pl.when(n == k)
            def _():
                slots[k, 0] = jnp.zeros((128, cols), F32)
            copy(k, 1, k).wait_recv()
            copy(k, 1, n).wait_send()
            total += slots[k, 0] + slots[k, 1]
        return total

    def ladder_out():
        total = acc[pl.ds(pl.multiple_of(n * 128, 128), 128), :]
        for k in range(4):
            @pl.when(n != k)
            def _():
                l_copy(k, k).wait_recv()
                l_copy(k, n).wait_send()

            @pl.when(n == k)
            def _():
                rs_l[k] = jnp.zeros((128, cols), F32)
            total += rs_l[k]
        out_ref[0] = total

    @pl.when(s == steps - 1)
    def _():
        last = depth - (steps - 1) * tk
        a = tau_ref[...]
        a = jnp.where(lax.broadcasted_iota(jnp.int32, a.shape, 0) < last, a, 0.0)
        b = vv_ref[...]
        b = jnp.where(lax.broadcasted_iota(jnp.int32, b.shape, 0) < last, b, 0.0)
        ladder(a, b)

        acc[...] = acc_t[...].T
        for k in range(4):
            @pl.when(n != k)
            def _():
                l_copy(k, n).start()

        yb_q().wait_recv()

        @pl.when(end)
        def _():
            be(1).start()

        split_b(b_q, b_hi, b_lo, kp, kq)
        yb_p().wait_recv()
        split_b(b_p, b_hi, b_lo, 0, kp)

        @pl.when(end)
        def _():
            end_block(z)
            for j in range(2):
                pe(zn, j).wait_recv()
            end_block(zn)
            for j in range(2):
                pe(zx, j).wait_recv()
            ladder_out()
            for j in range(2):
                pe(zxn, j).wait_recv()
            end_block(zxn)
            end_block(zx)
            total = gathered(part, rs_c, c_copy)
            f_copy().wait_recv()
            out_ref[1] = total + fin_r[...]
            for j in range(2):
                pe(z, j).wait_send()
                qe(z, j).wait_send()
                be(j).wait_send()

        @pl.when(mid)
        def _():
            px(zxn, 1).wait_recv()
            pe(zxn, 1).start()
            mid_block(z)
            mid_block(zn)
            for j in range(2):
                qx(zx, j).wait_recv()
            mid_block(zx)
            ladder_out()
            for j in range(2):
                be(j).wait_recv()
            split_b(be_q, e_hi, e_lo, 0, kq)
            far_block(z)
            far_block(zn)
            far_block(zx)
            for j in range(2):
                qx(zxn, j).wait_recv()
            far_block(zxn)
            mid_block(zxn)
            fin_s[...] = gathered(part_e, rs_e, e_copy)
            f_copy().start()
            out_ref[1] = gathered(part, rs_c, c_copy)
            for j in range(2):
                for k in (z, zx, zxn):
                    pe(k, j).wait_send()
                for k in (z, zn):
                    px(k, j).wait_send()
                    qx(k, j).wait_send()
            f_copy().wait_send()

        ya_p().wait_send()
        ya_q().wait_send()
        yb_p().wait_send()
        yb_q().wait_send()


def fused(tau, vv_integrals, cycle_amps, ov_integrals):
    depth = tau.shape[1]
    cols = vv_integrals.shape[1]
    rows, own = cycle_amps.shape
    tiles = -(-own // 256)
    kp = (tiles * 7 // 12) * 128
    kq = tiles * 128 - kp
    kh = kp + kq
    tk = 1280
    steps = -(-depth // tk)
    sem = pltpu.SemaphoreType.DMA
    both = pl.pallas_call(
        functools.partial(kernel, depth, tk, steps, kp, kq),
        grid=(steps,),
        out_shape=jax.ShapeDtypeStruct((2, 128, cols), F32),
        in_specs=[
            pl.BlockSpec((tk, tau.shape[0]), lambda s: (s, 0)),
            pl.BlockSpec((tk, cols), lambda s: (s, 0)),
            pl.BlockSpec((rows, own), lambda s: (0, 0)),
            pl.BlockSpec((own, cols), lambda s: (0, 0)),
        ],
        out_specs=pl.BlockSpec((2, 128, cols), lambda s: (0, 0, 0)),
        scratch_shapes=[
            pltpu.VMEM((4, 2, rows, kp), F32),
            pltpu.VMEM((4, 2, rows, kq), F32),
            pltpu.VMEM((rows, kp), F32),
            pltpu.VMEM((rows, kq), F32),
            pltpu.VMEM((2, kp, cols), F32),
            pltpu.VMEM((2, kq, cols), F32),
            pltpu.VMEM((kp, cols), F32),
            pltpu.VMEM((kq, cols), F32),
            pltpu.VMEM((2, kq, cols), F32),
            pltpu.VMEM((kh, 2 * cols), BF16),
            pltpu.VMEM((kh, 2 * cols), BF16),
            pltpu.VMEM((kq, 2 * cols), BF16),
            pltpu.VMEM((kq, 2 * cols), BF16),
            pltpu.VMEM((cols, 512), F32),
            pltpu.VMEM((512, cols), F32),
            pltpu.VMEM((4, 2, 128, cols), F32),
            pltpu.VMEM((4, 2, 128, cols), F32),
            pltpu.VMEM((4, 2, 128, cols), F32),
            pltpu.VMEM((4, 2, 128, cols), F32),
            pltpu.VMEM((4, 128, cols), F32),
            pltpu.VMEM((128, cols), F32),
            pltpu.VMEM((128, cols), F32),
            sem((4, 2)), sem((4, 2)), sem((4, 2)), sem((4, 2)), sem((4, 2)), sem((4, 2)),
            sem((4,)), sem((2,)), sem((2,)), sem((2,)),
            sem((4, 2)), sem((4, 2)), sem((4, 2)), sem((4, 2)), sem((4,)), sem((4,)), sem, sem,
        ],
        compiler_params=pltpu.CompilerParams(
            collective_id=0, has_side_effects=True, vmem_limit_bytes=56 * 1024 * 1024,
            dimension_semantics=("arbitrary",)),
        cost_estimate=pl.CostEstimate(flops=6 * 512 * depth * cols, bytes_accessed=4 * 512 * depth, transcendentals=0),
    )(tau.T, vv_integrals, cycle_amps, ov_integrals)
    return both[0], both[1]


def contract(left, right):
    return jnp.dot(left, right, precision=lax.Precision.HIGHEST, preferred_element_type=F32)


def plain(tau, vv_integrals, cycle_amps, ov_integrals):
    ladder_terms = contract(tau, vv_integrals)
    ladder_residual = lax.psum_scatter(ladder_terms, "narrow", scatter_dimension=0, tiled=True)
    cycle_terms = contract(lax.all_gather(cycle_amps, "wide", axis=0, tiled=True), ov_integrals)
    cycle_residual = lax.psum_scatter(cycle_terms, "narrow", scatter_dimension=0, tiled=True)
    return (ladder_residual, cycle_residual)


def solution(mesh):
    in_specs = (P(None, "narrow"), P("narrow", "wide"), P("wide", "narrow"), P("narrow", "wide"))
    out_specs = (P("narrow", "wide"), P("narrow", "wide"))
    small = mesh.shape["wide"] == 8 and mesh.shape["narrow"] == 4
    return jax.shard_map(fused if small else plain, mesh=mesh, in_specs=in_specs, out_specs=out_specs, check_vma=False)
```
